32 devices in a mesh: row: 4 (over x, core), col: 8 (over z, y).
Axes of the slice: x: 2, y: 2, z: 4, core: 2. Of those that a mesh axis runs over, the one named last changes fastest.
Arguments:
- jac: bfloat16 [768, 16384], P(('row', 'col')), may hold values from -0.21875 to 0.21875
- owner_list: int32 [768, 1], replicated, may hold values from 0 to 7; in each aligned block of 24 rows (0 to 23, 24 to 47, ...) at most 6 rows name the same one
- block_id: int32 [768], replicated, may hold values from 0 to 7
- diag_weight: float32 [64], replicated, may hold values from 0.25 to 4
- corr_weight: float32 [64], replicated, may hold values from 0.1 to 1
Outputs:
- gn_matrix: float32 [16384, 16384], P('row', 'col')
The draws below stay inside these ranges and needn't reach their ends.
Inputs may be any that keep to these rules, and one draw needn't show every extreme that they name: `owner_list`: among the 24 points of one mesh owner (aligned blocks of rows) no panel owner is named more than 6 times, and in some block one is named exactly 6 times.
All inputs are finite; a program needn't handle non-finite values.
Results may differ from the reference program's by a relative error of at most 0.0039.
Values may be sent and summed in bfloat16 or wider, within the bound.
A program may use at most 128 MiB of HBM per device.

```python
import math
import jax
import jax.numpy as jnp
import numpy as np

P_SIZE = 16384
PT_DEV = 24
BPC = 8
CAP = 6
POINTS = 768
NB = 64
N_COL = 8


def with_ends(array, key, least, high):
    spot = [jax.random.randint(jax.random.fold_in(key, axis), (), 0, length) for axis, length in enumerate(array.shape)]
    longest = array.shape.index(max(array.shape))
    neighbour = spot[:longest] + [(spot[longest] + 1) % array.shape[longest]] + spot[longest + 1:]
    return array.at[tuple(spot)].set(least).at[tuple(neighbour)].set(high)


def block_scale(own_key, dims, pieces, smallest, top_value):
    def one(dim, parts):
        draws = jax.random.uniform(jax.random.fold_in(jax.random.fold_in(own_key, 6), dim), (parts,), jnp.float32, smallest / len(pieces), top_value / len(pieces))
        return jnp.repeat(jnp.exp(draws), dims[dim] // parts).reshape((-1,) + (1,) * (len(dims) - dim - 1))

    gain = one(*pieces[0])
    for cut in pieces[1:]:
        gain = gain * one(*cut)
    return gain


def assign_block(stream_key, own, number, rows, count, top, reach, slope):
    sequence = jax.random.permutation(stream_key, count)
    packed, ordinary = portions_of(count, rows * top, reach, slope, True), portions_of(count, rows * top, reach, slope, False)
    places = jnp.arange(count)

    def named(tallies, turn):
        used = int((tallies > 0).sum())
        fixed = max(1, used // 4)
        passed = fixed + (places - fixed + turn * (used - fixed)) % max(1, count - fixed)
        return jnp.zeros((count,), jnp.int32).at[sequence[jnp.where(places < fixed, places, passed)]].set(jnp.asarray(tallies, jnp.int32))

    tallies = jnp.where(number % 4 == 0, named(packed, number // 4), named(ordinary, number - number // 4 - 1))
    mixed = jax.random.permutation(jax.random.fold_in(own, 3), count)
    giver, sink = mixed[0:count // 2 * 2:2], mixed[1:count // 2 * 2:2]
    slack = jnp.minimum(tallies[giver] - 1, reach - tallies[sink]) // 2
    slack = jnp.where((giver == sequence[0]) | (sink == sequence[0]) | (tallies[sink] == 0), 0, jnp.maximum(slack, 0))
    passed = jax.random.randint(jax.random.fold_in(own, 4), (count // 2,), 0, 1 << 20) % (slack + 1)
    tallies = tallies.at[giver].add(-passed).at[sink].add(passed)
    members = jnp.searchsorted(jnp.cumsum(tallies), jnp.arange(rows * top), side="right").astype(jnp.int32)
    listing = members.reshape(top, rows).T
    listing = listing[jax.random.permutation(jax.random.fold_in(own, 1), rows)]
    turn = jax.random.randint(jax.random.fold_in(own, 2), (rows, 1), 0, top)
    return jnp.take_along_axis(listing, (jnp.arange(top)[None, :] + turn) % top, axis=1)


def portions_of(amount, total, limit, slope, full):
    weights = [(1 << 20) // math.isqrt(standing ** slope) + 1 for standing in range(1, amount + 1)]
    largest = limit if full else min(limit, max(-(-total // amount), total * weights[0] // sum(weights)))
    least = 1 if total - largest >= amount - 1 else 0
    holding, spare = [largest] + [least] * (amount - 1), total - largest - least * (amount - 1)
    while spare > 0:
        candidates = [i for i in range(1, amount) if holding[i] < largest] or [i for i in range(1, amount) if holding[i] < limit]
        mass, left = sum([weights[i] for i in candidates]), spare
        for i in candidates:
            addition = min(limit - holding[i], max(1, left * weights[i] // mass), spare)
            holding[i] = holding[i] + addition
            spare = spare - addition
    return np.array(holding)


def gaussian(own_key, extent, scale, limit, cuts=(), kind=jnp.bfloat16):
    array = scale * jax.random.normal(own_key, extent, jnp.float32)
    if cuts:
        array = array * block_scale(own_key, extent, cuts, -0.22, 0.18)
    return jnp.clip(array, -limit, limit).astype(kind)


def setup_inputs(seed: int = 0) -> dict:
    arg_keys = jax.random.split(jax.random.key(seed), 6)
    jac = gaussian(arg_keys[0], (POINTS, P_SIZE), POINTS ** -0.5, 0.21875, ((0, 32),))
    owner_list_keys = jax.random.split(jax.random.fold_in(arg_keys[1], 1), POINTS // PT_DEV)
    owner_list_turns = jax.random.permutation(jax.random.fold_in(arg_keys[1], 3), POINTS // PT_DEV)
    owner_list = jax.vmap(lambda own, number: assign_block(jax.random.fold_in(arg_keys[1], 2), own, number, PT_DEV, N_COL, 1, CAP, 2))(owner_list_keys, owner_list_turns).reshape((POINTS, 1))
    block_id = with_ends(jax.random.randint(arg_keys[2], (POINTS,), 0, BPC), jax.random.fold_in(arg_keys[2], 1), 0, BPC - 1).astype(jnp.int32)
    diag_weight = jnp.clip(jnp.exp(jax.random.uniform(arg_keys[3], (NB,), jnp.float32, math.log(0.25), math.log(4.0))), 0.25, 4.0)
    corr_weight = jnp.clip(jnp.exp(jax.random.uniform(arg_keys[4], (NB,), jnp.float32, math.log(0.1), math.log(1.0))), 0.1, 1.0)
    return {"jac": jac, "owner_list": owner_list, "block_id": block_id, "diag_weight": diag_weight, "corr_weight": corr_weight}


def reference(jac, owner_list, block_id, diag_weight, corr_weight):
    group = (BPC * owner_list[:, 0] + block_id).astype(jnp.int32)
    wide = jac.astype(jnp.float32)
    block_sums = jax.ops.segment_sum(wide, group, num_segments=NB).astype(jnp.bfloat16)
    point_rows = (diag_weight[group][:, None] * wide).astype(jnp.bfloat16)
    block_rows = (corr_weight[:, None] * block_sums.astype(jnp.float32)).astype(jnp.bfloat16)
    first = jnp.dot(jac.T, point_rows, preferred_element_type=jnp.float32)
    second = jnp.dot(block_sums.T, block_rows, preferred_element_type=jnp.float32)
    return first + second
```

```python
import functools

import jax
import jax.numpy as jnp
from jax import lax
from jax.experimental import pallas as pl
from jax.experimental.pallas import tpu as pltpu
from jax.sharding import PartitionSpec as P

BPC = 8
MESH = pl.DeviceIdType.MESH


def gather_kernel(n_col, block, win, jac, a, w, loc, s1, ra, rw, sr, sl, sy, sw, sx, so):
    length = n_col // 2
    r, c = lax.axis_index("row"), lax.axis_index("col")
    z, y = c // 2, c % 2
    r1 = r + 1 - 2 * (r % 2)
    r2 = (r + 2) % 4
    r3 = (r1 + 2) % 4
    root = c // (block // win)
    root1 = root + 1 - 2 * (root % 2)
    root2 = (root + 2) % 4
    off = pl.multiple_of((c % (block // win)) * win, win)
    is_root, is_relay = r == root, r == root2
    has_right, has_left = z < length - 1, z > 0
    right, left, across = c + 2, c - 2, c + 1 - 2 * y

    barrier = pltpu.get_barrier_semaphore()

    def greet(row, col):
        pl.semaphore_signal(barrier, inc=1, device_id=(row, col), device_id_type=MESH)

    for peer in (r1, r2, r3):
        greet(peer, c)
    greet(r, across)

    @pl.when(has_right)
    def _():
        greet(r, right)

    @pl.when(has_left)
    def _():
        greet(r, left)

    pl.semaphore_wait(barrier, 4 + jnp.where(has_right, 1, 0) + jnp.where(has_left, 1, 0))

    def remote(src, dst, send, recv, row, col):
        return pltpu.make_async_remote_copy(
            src_ref=src, dst_ref=dst, send_sem=send, recv_sem=recv, device_id=(row, col), device_id_type=MESH
        )

    mine = c * 4 + r
    own = pltpu.make_async_copy(jac.at[:, pl.ds(pl.multiple_of(r * block, block), block)], a.at[mine], loc)
    own.start()
    first = [
        remote(jac.at[:, pl.ds(pl.multiple_of(peer * block, block), block)], a.at[mine], s1.at[i], ra.at[mine], peer, c)
        for i, peer in enumerate((r1, r2, r3))
    ]
    for copy in (first[1], first[2], first[0]):
        copy.start()

    def a_copy(s, sems, col):
        return remote(a.at[s], a.at[s], sems.at[s // 8 * 4 + s % 4], ra.at[s], r, col)

    def a_wait(s):
        a_copy(s, sy, across).wait_recv()

    def w_copy(s, sems, row):
        return remote(a.at[s, :, pl.ds(off, win)], w.at[s], sems.at[s], rw.at[s], row, c)

    def w_own(s):
        return pltpu.make_async_copy(a.at[s, :, pl.ds(off, win)], w.at[s], so.at[s])

    def w_relay(s):
        return remote(w.at[s], w.at[s], sw.at[s], rw.at[s], r1, c)

    def w_start(s):
        @pl.when(is_root)
        def _():
            w_copy(s, sx, root2).start()
            w_copy(s, sw, root1).start()
            w_own(s).start()

    def w_pass(s):
        @pl.when(is_relay)
        def _():
            w_relay(s).wait_recv()
            w_relay(s).start()

    def send_right(s):
        @pl.when(has_right)
        def _():
            a_copy(s, sr, right).start()

    def send_left(s):
        @pl.when(has_left)
        def _():
            a_copy(s, sl, left).start()

    def send_across(s):
        a_copy(s, sy, across).start()

    for j, k in enumerate((r, r1, r2, r3)):
        s = c * 4 + k
        if j == 0:
            own.wait()
        else:
            a_wait(s)
        send_right(s)
        send_left(s)
        send_across(s)
        w_start(s)

    def both(d, k, lane, act_left, act_right, first_too):
        @pl.when((d >= (0 if first_too else 1)) & (d < length) & (z - d >= 0))
        def _():
            act_left(((z - d) * 2 + lane) * 4 + k)

        @pl.when((d >= 1) & (d < length) & (z + d < length))
        def _():
            act_right(((z + d) * 2 + lane) * 4 + k)

    def step(t, carry):
        d, j = t // 4, t % 4
        k = jnp.where(j == 0, r, jnp.where(j == 1, r1, jnp.where(j == 2, r2, r3)))

        def from_left(s):
            a_wait(s)
            send_right(s)
            send_across(s)
            w_start(s)

        def from_right(s):
            a_wait(s)
            send_left(s)
            send_across(s)
            w_start(s)

        def from_across(s):
            a_wait(s)
            w_start(s)

        both(d, k, y, from_left, from_right, False)
        both(d - 1, k, 1 - y, from_across, from_across, True)
        both(d - 1, k, y, w_pass, w_pass, True)
        both(d - 2, k, 1 - y, w_pass, w_pass, True)
        return carry

    lax.fori_loop(4, (length + 2) * 4, step, 0)

    def finish(i, carry):
        zz, k = i // 4, i % 4
        s = (zz * 2 + y) * 4 + k
        a_copy(s, sy, across).wait_send()

        @pl.when(has_right & (zz <= z))
        def _():
            a_copy(s, sr, right).wait_send()

        @pl.when(has_left & (zz >= z))
        def _():
            a_copy(s, sl, left).wait_send()

        return carry

    lax.fori_loop(0, length * 4, finish, 0)

    def finish_w(s, carry):
        @pl.when(is_root)
        def _():
            w_copy(s, sx, root2).wait_send()
            w_copy(s, sw, root1).wait_send()
            w_own(s).wait()

        @pl.when(is_relay)
        def _():
            w_relay(s).wait_send()

        @pl.when(jnp.logical_not(is_root | is_relay))
        def _():
            w_relay(s).wait_recv()

        return carry

    lax.fori_loop(0, n_col * 4, finish_w, 0)
    for copy in first:
        copy.wait_send()


def product_kernel(g_col, g_row, diag, corr, a, w, out, scaled):
    points, win = w.shape
    nblocks = corr.shape[0]

    @pl.when(pl.program_id(0) == 0)
    def _():
        hit = g_col[...] == lax.broadcasted_iota(jnp.int32, (points, nblocks), 1)
        scale = jnp.sum(jnp.where(hit, diag[...], 0.0), axis=1, keepdims=True)
        spread = jnp.where(hit, 1.0, 0.0).astype(jnp.bfloat16)
        member = jnp.where(g_row[...] == lax.broadcasted_iota(jnp.int32, (nblocks, points), 0), 1.0, 0.0).astype(
            jnp.bfloat16
        )

        @pl.loop(0, win // 256)
        def _(i):
            cols = pl.ds(pl.multiple_of(i * 256, 256), 256)
            part = w[:, cols]
            sums = jnp.dot(member, part, preferred_element_type=jnp.float32).astype(jnp.bfloat16)
            rows = (corr[...] * sums.astype(jnp.float32)).astype(jnp.bfloat16)
            back = jnp.dot(spread, rows, preferred_element_type=jnp.float32)
            scaled[:, cols] = (scale * part.astype(jnp.float32) + back).astype(jnp.bfloat16)

    out[...] = lax.dot_general(
        a[...], scaled[...], (((0,), (0,)), ((), ())), preferred_element_type=jnp.float32
    )


def local(jac, owner_list, block_id, diag_weight, corr_weight):
    n_row, n_col = lax.axis_size("row"), lax.axis_size("col")
    pt_dev, width = jac.shape
    points = owner_list.shape[0]
    block, win = width // n_row, width // n_col
    slots = n_row * n_col
    nblocks = diag_weight.shape[0]
    dma = pltpu.SemaphoreType.DMA
    a, w = pl.pallas_call(
        functools.partial(gather_kernel, n_col, block, win),
        out_shape=(
            jax.ShapeDtypeStruct((slots, pt_dev, block), jac.dtype),
            jax.ShapeDtypeStruct((slots, pt_dev, win), jac.dtype),
        ),
        in_specs=[pl.BlockSpec(memory_space=pl.ANY)],
        out_specs=(pl.BlockSpec(memory_space=pl.ANY), pl.BlockSpec(memory_space=pl.ANY)),
        scratch_shapes=[
            dma(()), dma((3,)), dma((slots,)), dma((slots,)), dma((slots // 2,)), dma((slots // 2,)),
            dma((slots // 2,)), dma((slots,)), dma((slots,)), dma((slots,)),
        ],
        compiler_params=pltpu.CompilerParams(collective_id=0, has_side_effects=True),
        name="gather",
    )(jac)
    a = a.reshape(points, block)
    w = w.reshape(points, win)
    group = owner_list[:, 0] * BPC + block_id
    group = group.reshape(n_row, n_col, pt_dev).transpose(1, 0, 2).reshape(points)
    tile = 512
    whole = lambda *shape: pl.BlockSpec(shape, lambda i: (0, 0))
    return pl.pallas_call(
        product_kernel,
        grid=(block // tile,),
        out_shape=jax.ShapeDtypeStruct((block, win), jnp.float32),
        in_specs=[
            whole(points, 1), whole(1, points), whole(1, nblocks), whole(nblocks, 1),
            pl.BlockSpec((points, tile), lambda i: (0, i)), whole(points, win),
        ],
        out_specs=pl.BlockSpec((tile, win), lambda i: (i, 0)),
        scratch_shapes=[pltpu.VMEM((points, win), jnp.bfloat16)],
        compiler_params=pltpu.CompilerParams(vmem_limit_bytes=56 * 1024 * 1024),
        cost_estimate=pl.CostEstimate(flops=2 * points * block * win, bytes_accessed=4 * block * win, transcendentals=0),
        name="product",
    )(group[:, None], group[None, :], diag_weight[None, :], corr_weight[:, None], a, w)


def solution(mesh):
    in_specs = (P(("row", "col"), None), P(), P(), P(), P())
    out_specs = P("row", "col")
    return jax.shard_map(local, mesh=mesh, in_specs=in_specs, out_specs=out_specs, check_vma=False)
```

```python
import functools

import jax
import jax.numpy as jnp
from jax import lax
from jax.experimental import pallas as pl
from jax.experimental.pallas import tpu as pltpu
from jax.sharding import PartitionSpec as P

BPC = 8
MESH = pl.DeviceIdType.MESH


def gather_kernel(n_col, block, win, jac, a, w, loc, s1, ra, rw, sr, sl, sy, sw, sx):
    length = n_col // 2
    r, c = lax.axis_index("row"), lax.axis_index("col")
    z, y = c // 2, c % 2
    r1 = r + 1 - 2 * (r % 2)
    r2 = (r + 2) % 4
    r3 = (r1 + 2) % 4
    root = c // (block // win)
    root1 = root + 1 - 2 * (root % 2)
    root2 = (root + 2) % 4
    off = pl.multiple_of((c % (block // win)) * win, win)
    is_root, is_relay = r == root, r == root2
    has_right, has_left = z < length - 1, z > 0
    right, left, across = c + 2, c - 2, c + 1 - 2 * y

    barrier = pltpu.get_barrier_semaphore()

    def greet(row, col):
        pl.semaphore_signal(barrier, inc=1, device_id=(row, col), device_id_type=MESH)

    for peer in (r1, r2, r3):
        greet(peer, c)
    greet(r, across)

    @pl.when(has_right)
    def _():
        greet(r, right)

    @pl.when(has_left)
    def _():
        greet(r, left)

    pl.semaphore_wait(barrier, 4 + jnp.where(has_right, 1, 0) + jnp.where(has_left, 1, 0))

    def remote(src, dst, send, recv, row, col):
        return pltpu.make_async_remote_copy(
            src_ref=src, dst_ref=dst, send_sem=send, recv_sem=recv, device_id=(row, col), device_id_type=MESH
        )

    mine = r * n_col + c
    own = pltpu.make_async_copy(jac.at[:, pl.ds(pl.multiple_of(r * block, block), block)], a.at[mine], loc)
    own.start()
    first = [
        remote(jac.at[:, pl.ds(pl.multiple_of(peer * block, block), block)], a.at[mine], s1.at[i], ra.at[mine], peer, c)
        for i, peer in enumerate((r1, r2, r3))
    ]
    for copy in (first[1], first[2], first[0]):
        copy.start()

    def a_copy(s, sems, col):
        return remote(a.at[s], a.at[s], sems.at[s % n_col // 2 * 4 + s // n_col], ra.at[s], r, col)

    def a_wait(s):
        a_copy(s, sy, across).wait_recv()

    def w_copy(s, sems, row):
        return remote(a.at[s, :, pl.ds(off, win)], w.at[s], sems.at[s], rw.at[s], row, c)

    def w_relay(s):
        return remote(w.at[s], w.at[s], sw.at[s], rw.at[s], r1, c)

    def w_start(s):
        @pl.when(is_root)
        def _():
            w_copy(s, sx, root2).start()
            w_copy(s, sw, root1).start()

    def w_pass(s):
        @pl.when(is_relay)
        def _():
            w_relay(s).wait_recv()
            w_relay(s).start()

    def send_right(s):
        @pl.when(has_right)
        def _():
            a_copy(s, sr, right).start()

    def send_left(s):
        @pl.when(has_left)
        def _():
            a_copy(s, sl, left).start()

    def send_across(s):
        a_copy(s, sy, across).start()

    for j, k in enumerate((r, r1, r2, r3)):
        s = k * n_col + c
        if j == 0:
            own.wait()
        else:
            a_wait(s)
        send_right(s)
        send_left(s)
        send_across(s)
        w_start(s)

    def both(d, k, lane, act_left, act_right, first_too):
        @pl.when((d >= (0 if first_too else 1)) & (d < length) & (z - d >= 0))
        def _():
            act_left(k * n_col + (z - d) * 2 + lane)

        @pl.when((d >= 1) & (d < length) & (z + d < length))
        def _():
            act_right(k * n_col + (z + d) * 2 + lane)

    def step(t, carry):
        d, j = t // 4, t % 4
        k = jnp.where(j == 0, r, jnp.where(j == 1, r1, jnp.where(j == 2, r2, r3)))

        def from_left(s):
            a_wait(s)
            send_right(s)
            send_across(s)
            w_start(s)

        def from_right(s):
            a_wait(s)
            send_left(s)
            send_across(s)
            w_start(s)

        def from_across(s):
            a_wait(s)
            w_start(s)

        both(d, k, y, from_left, from_right, False)
        both(d - 1, k, 1 - y, from_across, from_across, True)
        both(d - 1, k, y, w_pass, w_pass, True)
        both(d - 2, k, 1 - y, w_pass, w_pass, True)
        return carry

    lax.fori_loop(4, (length + 2) * 4, step, 0)

    def finish(i, carry):
        zz, k = i // 4, i % 4
        s = k * n_col + zz * 2 + y
        a_copy(s, sy, across).wait_send()

        @pl.when(has_right & (zz <= z))
        def _():
            a_copy(s, sr, right).wait_send()

        @pl.when(has_left & (zz >= z))
        def _():
            a_copy(s, sl, left).wait_send()

        return carry

    lax.fori_loop(0, length * 4, finish, 0)

    def finish_w(s, carry):
        @pl.when(is_root)
        def _():
            w_copy(s, sx, root2).wait_send()
            w_copy(s, sw, root1).wait_send()

        @pl.when(is_relay)
        def _():
            w_relay(s).wait_send()

        @pl.when(jnp.logical_not(is_root | is_relay))
        def _():
            w_relay(s).wait_recv()

        return carry

    lax.fori_loop(0, n_col * 4, finish_w, 0)
    for copy in first:
        copy.wait_send()


def product_kernel(group, diag, corr, a, a_all, w_all, out, w, scaled, sem):
    points, win = w.shape
    nblocks = corr.shape[1]
    per_row = a_all.shape[1] // win

    @pl.when(pl.program_id(0) == 0)
    def _():
        r, c = lax.axis_index("row"), lax.axis_index("col")
        off = pl.multiple_of((c % per_row) * win, win)
        is_root = r == c // per_row

        @pl.when(is_root)
        def _():
            pltpu.make_async_copy(a_all.at[:, pl.ds(off, win)], w, sem).start()

        @pl.when(jnp.logical_not(is_root))
        def _():
            pltpu.make_async_copy(w_all, w, sem).start()

        block = lax.broadcasted_iota(jnp.int32, (nblocks, points), 0)
        member = jnp.where(group[...] == block, 1.0, 0.0)
        spread = member.T
        scale = jnp.sum(spread * diag[...], axis=1, keepdims=True)
        member, spread = member.astype(jnp.bfloat16), spread.astype(jnp.bfloat16)
        square = (nblocks, nblocks)
        same = lax.broadcasted_iota(jnp.int32, square, 0) == lax.broadcasted_iota(jnp.int32, square, 1)
        weight = jnp.sum(jnp.where(same, corr[...], 0.0), axis=1, keepdims=True)
        pltpu.make_async_copy(w_all, w, sem).wait()
        wide = min(win, 512)
        for i in range(win // wide):
            cols = slice(i * wide, (i + 1) * wide)
            part = w[:, cols]
            sums = jnp.dot(member, part, preferred_element_type=jnp.float32).astype(jnp.bfloat16)
            rows = (weight * sums.astype(jnp.float32)).astype(jnp.bfloat16)
            back = jnp.dot(spread, rows, preferred_element_type=jnp.float32)
            scaled[:, cols] = (scale * part.astype(jnp.float32) + back).astype(jnp.bfloat16)

    out[...] = lax.dot_general(
        a[...], scaled[...], (((0,), (0,)), ((), ())), preferred_element_type=jnp.float32
    )


def local(jac, owner_list, block_id, diag_weight, corr_weight):
    n_row, n_col = lax.axis_size("row"), lax.axis_size("col")
    pt_dev, width = jac.shape
    points = owner_list.shape[0]
    block, win = width // n_row, width // n_col
    slots = n_row * n_col
    nblocks = diag_weight.shape[0]
    dma = pltpu.SemaphoreType.DMA
    a, w = pl.pallas_call(
        functools.partial(gather_kernel, n_col, block, win),
        out_shape=(
            jax.ShapeDtypeStruct((slots, pt_dev, block), jac.dtype),
            jax.ShapeDtypeStruct((slots, pt_dev, win), jac.dtype),
        ),
        in_specs=[pl.BlockSpec(memory_space=pl.ANY)],
        out_specs=(pl.BlockSpec(memory_space=pl.ANY), pl.BlockSpec(memory_space=pl.ANY)),
        scratch_shapes=[
            dma(()), dma((3,)), dma((slots,)), dma((slots,)), dma((slots // 2,)), dma((slots // 2,)),
            dma((slots // 2,)), dma((slots,)), dma((slots,)),
        ],
        compiler_params=pltpu.CompilerParams(collective_id=0, has_side_effects=True),
        name="gather",
    )(jac)
    a = a.reshape(points, block)
    w = w.reshape(points, win)
    group = owner_list.reshape(1, points) * BPC + block_id.reshape(1, points)
    tile = 512
    whole = lambda *shape: pl.BlockSpec(shape, lambda i: (0, 0))
    return pl.pallas_call(
        product_kernel,
        grid=(block // tile,),
        out_shape=jax.ShapeDtypeStruct((block, win), jnp.float32),
        in_specs=[
            whole(1, points), whole(1, nblocks), whole(1, nblocks),
            pl.BlockSpec((points, tile), lambda i: (0, i)),
            pl.BlockSpec(memory_space=pl.ANY), pl.BlockSpec(memory_space=pl.ANY),
        ],
        out_specs=pl.BlockSpec((tile, win), lambda i: (i, 0)),
        scratch_shapes=[pltpu.VMEM((points, win), jnp.bfloat16)] * 2 + [dma(())],
        compiler_params=pltpu.CompilerParams(vmem_limit_bytes=56 * 1024 * 1024),
        cost_estimate=pl.CostEstimate(flops=2 * points * block * win, bytes_accessed=4 * block * win, transcendentals=0),
        name="product",
    )(group, diag_weight[None, :], corr_weight[None, :], a, a, w)


def solution(mesh):
    in_specs = (P(("row", "col"), None), P(), P(), P(), P())
    out_specs = P("row", "col")
    return jax.shard_map(local, mesh=mesh, in_specs=in_specs, out_specs=out_specs, check_vma=False)
```

```python
import functools

import jax
import jax.numpy as jnp
from jax import lax
from jax.experimental import pallas as pl
from jax.experimental.pallas import tpu as pltpu
from jax.sharding import PartitionSpec as P

BPC = 8
MESH = pl.DeviceIdType.MESH


def gather_kernel(n_col, block, win, jac, a, w, loc, s1, sn, rn, rb, rw, nr, nl, sr, sl, sy, sw, sx):
    length = n_col // 2
    r, c = lax.axis_index("row"), lax.axis_index("col")
    z, y = c // 2, c % 2
    r1 = r + 1 - 2 * (r % 2)
    r2 = (r + 2) % 4
    r3 = (r1 + 2) % 4
    root = c // (block // win)
    root1 = root + 1 - 2 * (root % 2)
    root2 = (root + 2) % 4
    off = pl.multiple_of((c % (block // win)) * win, win)
    is_root, is_relay = r == root, r == root2
    has_right, has_left = z < length - 1, z > 0
    right, left, across = c + 2, c - 2, c + 1 - 2 * y

    barrier = pltpu.get_barrier_semaphore()

    def greet(row, col):
        pl.semaphore_signal(barrier, inc=1, device_id=(row, col), device_id_type=MESH)

    for peer in (r1, r2, r3):
        greet(peer, c)
    greet(r, across)

    @pl.when(has_right)
    def _():
        greet(r, right)

    @pl.when(has_left)
    def _():
        greet(r, left)

    pl.semaphore_wait(barrier, 4 + jnp.where(has_right, 1, 0) + jnp.where(has_left, 1, 0))

    def remote(src, dst, send, recv, row, col):
        return pltpu.make_async_remote_copy(
            src_ref=src, dst_ref=dst, send_sem=send, recv_sem=recv, device_id=(row, col), device_id_type=MESH
        )

    mine = r * n_col + c
    own = pltpu.make_async_copy(jac.at[:, pl.ds(pl.multiple_of(r * block, block), block)], a.at[mine], loc)
    own.start()
    first = [
        remote(jac.at[:, pl.ds(pl.multiple_of(peer * block, block), block)], a.at[mine], s1.at[i], rb.at[mine], peer, c)
        for i, peer in enumerate((r1, r2, r3))
    ]
    for copy in (first[1], first[2], first[0]):
        copy.start()

    cut = block * 5 // 32
    near, far = pl.ds(0, cut), pl.ds(cut, block - cut)

    def n_copy(s, send, col):
        return remote(a.at[s, :, near], a.at[s, :, near], send, rn.at[s], r, col)

    def n_across(s):
        return n_copy(s, sn.at[s // n_col], across)

    def n_right(s):
        return n_copy(s, nr.at[s], right)

    def n_left(s):
        return n_copy(s, nl.at[s], left)

    def a_copy(s, sems, col):
        return remote(
            a.at[s, :, far], a.at[s, :, far], sems.at[s % n_col // 2 * 4 + s // n_col], rb.at[s], r, col
        )

    def a_wait(s):
        a_copy(s, sy, across).wait_recv()

    def w_copy(s, sems, row):
        return remote(a.at[s, :, pl.ds(off, win)], w.at[s], sems.at[s], rw.at[s], row, c)

    def w_relay(s):
        return remote(w.at[s], w.at[s], sw.at[s], rw.at[s], r1, c)

    def w_start(s):
        @pl.when(is_root)
        def _():
            w_copy(s, sx, root2).start()
            w_copy(s, sw, root1).start()

    def w_pass(s):
        @pl.when(is_relay)
        def _():
            w_relay(s).wait_recv()
            w_relay(s).start()

    def send_right(s):
        @pl.when(has_right)
        def _():
            a_copy(s, sr, right).start()

    def send_left(s):
        @pl.when(has_left)
        def _():
            a_copy(s, sl, left).start()

    def near_right(s):
        @pl.when(has_right)
        def _():
            n_right(s).start()

    def near_left(s):
        @pl.when(has_left)
        def _():
            n_left(s).start()

    def send_across(s):
        a_copy(s, sy, across).start()

    for j, k in enumerate((r, r1, r2, r3)):
        s = k * n_col + c
        if j == 0:
            own.wait()
        else:
            remote(a.at[s], a.at[s], s1.at[0], rb.at[s], r1, c).wait_recv()
        n_across(s).start()
        send_right(s)
        send_left(s)
        send_across(s)
        near_right(s)
        near_left(s)
        w_start(s)

    def both(d, k, lane, act_left, act_right, first_too):
        @pl.when((d >= (0 if first_too else 1)) & (d < length) & (z - d >= 0))
        def _():
            act_left(k * n_col + (z - d) * 2 + lane)

        @pl.when((d >= 1) & (d < length) & (z + d < length))
        def _():
            act_right(k * n_col + (z + d) * 2 + lane)

    def step(t, carry):
        d, j = t // 4, t % 4
        k = jnp.where(j == 0, r, jnp.where(j == 1, r1, jnp.where(j == 2, r2, r3)))

        def from_left(s):
            a_wait(s)
            send_right(s)
            send_across(s)
            n_across(s).wait_recv()
            near_right(s)
            w_start(s)

        def from_right(s):
            a_wait(s)
            send_left(s)
            send_across(s)
            n_across(s).wait_recv()
            near_left(s)
            w_start(s)

        def near_from_left(s):
            n_across(s).wait_recv()
            near_right(s)

            @pl.when(d == 1)
            def _():
                near_left(s)

        def near_from_right(s):
            n_across(s).wait_recv()
            near_left(s)

        def from_across(s):
            a_wait(s)
            w_start(s)

        both(d, k, y, from_left, from_right, False)
        both(d - 1, k, 1 - y, near_from_left, near_from_right, True)
        both(d - 1, k, 1 - y, from_across, from_across, True)
        both(d - 1, k, y, w_pass, w_pass, True)
        both(d - 2, k, 1 - y, w_pass, w_pass, True)
        return carry

    lax.fori_loop(4, (length + 2) * 4, step, 0)

    def finish(i, carry):
        zz, k = i // 4, i % 4
        s = k * n_col + zz * 2 + y
        a_copy(s, sy, across).wait_send()

        @pl.when(has_right & (zz <= z))
        def _():
            a_copy(s, sr, right).wait_send()

        @pl.when(has_left & (zz >= z))
        def _():
            a_copy(s, sl, left).wait_send()

        return carry

    lax.fori_loop(0, length * 4, finish, 0)

    for k in range(4):
        n_across(k * n_col + c).wait_send()

    def finish_w(s, carry):
        zz = s % n_col // 2

        @pl.when(has_right & (zz <= z))
        def _():
            n_right(s).wait_send()

        @pl.when(has_left & (zz >= z))
        def _():
            n_left(s).wait_send()

        @pl.when(is_root)
        def _():
            w_copy(s, sx, root2).wait_send()
            w_copy(s, sw, root1).wait_send()

        @pl.when(is_relay)
        def _():
            w_relay(s).wait_send()

        @pl.when(jnp.logical_not(is_root | is_relay))
        def _():
            w_relay(s).wait_recv()

        return carry

    lax.fori_loop(0, n_col * 4, finish_w, 0)
    for copy in first:
        copy.wait_send()


def product_kernel(group, diag, corr, a, a_all, w_all, out, w, scaled, sem):
    points, win = w.shape
    nblocks = corr.shape[1]
    per_row = a_all.shape[1] // win

    @pl.when(pl.program_id(0) == 0)
    def _():
        r, c = lax.axis_index("row"), lax.axis_index("col")
        off = pl.multiple_of((c % per_row) * win, win)
        is_root = r == c // per_row

        @pl.when(is_root)
        def _():
            pltpu.make_async_copy(a_all.at[:, pl.ds(off, win)], w, sem).start()

        @pl.when(jnp.logical_not(is_root))
        def _():
            pltpu.make_async_copy(w_all, w, sem).start()

        block = lax.broadcasted_iota(jnp.int32, (nblocks, points), 0)
        member = jnp.where(group[...] == block, 1.0, 0.0)
        spread = member.T
        scale = jnp.sum(spread * diag[...], axis=1, keepdims=True)
        member, spread = member.astype(jnp.bfloat16), spread.astype(jnp.bfloat16)
        square = (nblocks, nblocks)
        same = lax.broadcasted_iota(jnp.int32, square, 0) == lax.broadcasted_iota(jnp.int32, square, 1)
        weight = jnp.sum(jnp.where(same, corr[...], 0.0), axis=1, keepdims=True)
        pltpu.make_async_copy(w_all, w, sem).wait()
        wide = min(win, 512)
        for i in range(win // wide):
            cols = slice(i * wide, (i + 1) * wide)
            part = w[:, cols]
            sums = jnp.dot(member, part, preferred_element_type=jnp.float32).astype(jnp.bfloat16)
            rows = (weight * sums.astype(jnp.float32)).astype(jnp.bfloat16)
            back = jnp.dot(spread, rows, preferred_element_type=jnp.float32)
            scaled[:, cols] = (scale * part.astype(jnp.float32) + back).astype(jnp.bfloat16)

    out[...] = lax.dot_general(
        a[...], scaled[...], (((0,), (0,)), ((), ())), preferred_element_type=jnp.float32
    )


def local(jac, owner_list, block_id, diag_weight, corr_weight):
    n_row, n_col = lax.axis_size("row"), lax.axis_size("col")
    pt_dev, width = jac.shape
    points = owner_list.shape[0]
    block, win = width // n_row, width // n_col
    slots = n_row * n_col
    nblocks = diag_weight.shape[0]
    dma = pltpu.SemaphoreType.DMA
    a, w = pl.pallas_call(
        functools.partial(gather_kernel, n_col, block, win),
        out_shape=(
            jax.ShapeDtypeStruct((slots, pt_dev, block), jac.dtype),
            jax.ShapeDtypeStruct((slots, pt_dev, win), jac.dtype),
        ),
        in_specs=[pl.BlockSpec(memory_space=pl.ANY)],
        out_specs=(pl.BlockSpec(memory_space=pl.ANY), pl.BlockSpec(memory_space=pl.ANY)),
        scratch_shapes=[
            dma(()), dma((3,)), dma((n_row,)), dma((slots,)), dma((slots,)), dma((slots,)), dma((slots,)), dma((slots,)),
            dma((slots // 2,)), dma((slots // 2,)), dma((slots // 2,)), dma((slots,)), dma((slots,)),
        ],
        compiler_params=pltpu.CompilerParams(collective_id=0, has_side_effects=True),
        name="gather",
    )(jac)
    a = a.reshape(points, block)
    w = w.reshape(points, win)
    group = owner_list.reshape(1, points) * BPC + block_id.reshape(1, points)
    tile = 512
    whole = lambda *shape: pl.BlockSpec(shape, lambda i: (0, 0))
    return pl.pallas_call(
        product_kernel,
        grid=(block // tile,),
        out_shape=jax.ShapeDtypeStruct((block, win), jnp.float32),
        in_specs=[
            whole(1, points), whole(1, nblocks), whole(1, nblocks),
            pl.BlockSpec((points, tile), lambda i: (0, i)),
            pl.BlockSpec(memory_space=pl.ANY), pl.BlockSpec(memory_space=pl.ANY),
        ],
        out_specs=pl.BlockSpec((tile, win), lambda i: (i, 0)),
        scratch_shapes=[pltpu.VMEM((points, win), jnp.bfloat16)] * 2 + [dma(())],
        compiler_params=pltpu.CompilerParams(vmem_limit_bytes=56 * 1024 * 1024),
        cost_estimate=pl.CostEstimate(flops=2 * points * block * win, bytes_accessed=4 * block * win, transcendentals=0),
        name="product",
    )(group, diag_weight[None, :], corr_weight[None, :], a, a, w)


def solution(mesh):
    in_specs = (P(("row", "col"), None), P(), P(), P(), P())
    out_specs = P("row", "col")
    return jax.shard_map(local, mesh=mesh, in_specs=in_specs, out_specs=out_specs, check_vma=False)
```

```python
import functools

import jax
import jax.numpy as jnp
from jax import lax
from jax.experimental import pallas as pl
from jax.experimental.pallas import tpu as pltpu
from jax.sharding import PartitionSpec as P

BPC = 8
MESH = pl.DeviceIdType.MESH


def gather_kernel(n_col, block, win, jac, a, w, loc, s1, sn, rn, rb, rw, nr, nl, sr, sl, sy, sw, sx):
    length = n_col // 2
    r, c = lax.axis_index("row"), lax.axis_index("col")
    z, y = c // 2, c % 2
    r1 = r + 1 - 2 * (r % 2)
    r2 = (r + 2) % 4
    r3 = (r1 + 2) % 4
    root = c // (block // win)
    root1 = root + 1 - 2 * (root % 2)
    root2 = (root + 2) % 4
    off = pl.multiple_of((c % (block // win)) * win, win)
    is_root, is_relay = r == root, r == root2
    has_right, has_left = z < length - 1, z > 0
    right, left, across = c + 2, c - 2, c + 1 - 2 * y

    barrier = pltpu.get_barrier_semaphore()

    def greet(row, col):
        pl.semaphore_signal(barrier, inc=1, device_id=(row, col), device_id_type=MESH)

    for peer in (r1, r2, r3):
        greet(peer, c)
    greet(r, across)

    @pl.when(has_right)
    def _():
        greet(r, right)

    @pl.when(has_left)
    def _():
        greet(r, left)

    pl.semaphore_wait(barrier, 4 + jnp.where(has_right, 1, 0) + jnp.where(has_left, 1, 0))

    def remote(src, dst, send, recv, row, col):
        return pltpu.make_async_remote_copy(
            src_ref=src, dst_ref=dst, send_sem=send, recv_sem=recv, device_id=(row, col), device_id_type=MESH
        )

    mine = r * n_col + c
    own = pltpu.make_async_copy(jac.at[:, pl.ds(pl.multiple_of(r * block, block), block)], a.at[mine], loc)
    own.start()
    first = [
        remote(jac.at[:, pl.ds(pl.multiple_of(peer * block, block), block)], a.at[mine], s1.at[i], rb.at[mine], peer, c)
        for i, peer in enumerate((r1, r2, r3))
    ]
    for copy in (first[1], first[2], first[0]):
        copy.start()

    cut = block * 5 // 32
    near, far = pl.ds(0, cut), pl.ds(cut, block - cut)

    def n_copy(s, send, col):
        return remote(a.at[s, :, near], a.at[s, :, near], send, rn.at[s], r, col)

    def n_across(s):
        return n_copy(s, sn.at[s // n_col], across)

    def n_right(s):
        return n_copy(s, nr.at[s], right)

    def n_left(s):
        return n_copy(s, nl.at[s], left)

    def a_copy(s, sems, col):
        return remote(
            a.at[s, :, far], a.at[s, :, far], sems.at[s % n_col // 2 * 4 + s // n_col], rb.at[s], r, col
        )

    def a_wait(s):
        a_copy(s, sy, across).wait_recv()

    def w_copy(s, sems, row):
        return remote(a.at[s, :, pl.ds(off, win)], w.at[s], sems.at[s], rw.at[s], row, c)

    def w_relay(s):
        return remote(w.at[s], w.at[s], sw.at[s], rw.at[s], r1, c)

    def w_start(s):
        @pl.when(is_root)
        def _():
            w_copy(s, sx, root2).start()
            w_copy(s, sw, root1).start()

    def w_pass(s):
        @pl.when(is_relay)
        def _():
            w_relay(s).wait_recv()
            w_relay(s).start()

    def send_right(s):
        @pl.when(has_right)
        def _():
            a_copy(s, sr, right).start()

    def send_left(s):
        @pl.when(has_left)
        def _():
            a_copy(s, sl, left).start()

    def near_right(s):
        @pl.when(has_right)
        def _():
            n_right(s).start()

    def near_left(s):
        @pl.when(has_left)
        def _():
            n_left(s).start()

    def send_across(s):
        a_copy(s, sy, across).start()

    for j, k in enumerate((r, r1, r2, r3)):
        s = k * n_col + c
        if j == 0:
            own.wait()
        else:
            remote(a.at[s], a.at[s], s1.at[0], rb.at[s], r1, c).wait_recv()
        n_across(s).start()
        send_right(s)
        send_left(s)
        send_across(s)
        near_right(s)
        near_left(s)
        w_start(s)

    def both(d, k, lane, act_left, act_right, first_too):
        @pl.when((d >= (0 if first_too else 1)) & (d < length) & (z - d >= 0))
        def _():
            act_left(k * n_col + (z - d) * 2 + lane)

        @pl.when((d >= 1) & (d < length) & (z + d < length))
        def _():
            act_right(k * n_col + (z + d) * 2 + lane)

    def step(t, carry):
        d, j = t // 4, t % 4
        k = jnp.where(j == 0, r, jnp.where(j == 1, r1, jnp.where(j == 2, r2, r3)))

        def from_left(s):
            a_wait(s)
            send_right(s)
            send_across(s)
            n_across(s).wait_recv()
            near_right(s)
            w_start(s)

        def from_right(s):
            a_wait(s)
            send_left(s)
            send_across(s)
            n_across(s).wait_recv()
            near_left(s)
            w_start(s)

        def near_from_left(s):
            n_across(s).wait_recv()
            near_right(s)

            @pl.when(d == 1)
            def _():
                near_left(s)

        def near_from_right(s):
            n_across(s).wait_recv()
            near_left(s)

        def from_across(s):
            a_wait(s)
            w_start(s)

        both(d, k, y, from_left, from_right, False)
        both(d - 1, k, 1 - y, near_from_left, near_from_right, True)
        both(d - 1, k, 1 - y, from_across, from_across, True)
        both(d - 1, k, y, w_pass, w_pass, True)
        both(d - 2, k, 1 - y, w_pass, w_pass, True)
        return carry

    lax.fori_loop(4, (length + 2) * 4, step, 0)

    def finish(i, carry):
        zz, k = i // 4, i % 4
        s = k * n_col + zz * 2 + y
        a_copy(s, sy, across).wait_send()

        @pl.when(has_right & (zz <= z))
        def _():
            a_copy(s, sr, right).wait_send()

        @pl.when(has_left & (zz >= z))
        def _():
            a_copy(s, sl, left).wait_send()

        return carry

    lax.fori_loop(0, length * 4, finish, 0)

    for k in range(4):
        n_across(k * n_col + c).wait_send()

    def finish_w(s, carry):
        zz = s % n_col // 2

        @pl.when(has_right & (zz <= z))
        def _():
            n_right(s).wait_send()

        @pl.when(has_left & (zz >= z))
        def _():
            n_left(s).wait_send()

        @pl.when(is_root)
        def _():
            w_copy(s, sx, root2).wait_send()
            w_copy(s, sw, root1).wait_send()

        @pl.when(is_relay)
        def _():
            w_relay(s).wait_send()

        @pl.when(jnp.logical_not(is_root | is_relay))
        def _():
            w_relay(s).wait_recv()

        return carry

    lax.fori_loop(0, n_col * 4, finish_w, 0)
    for copy in first:
        copy.wait_send()


def product_kernel(group, diag, corr, a, a_all, w_all, out, w, scaled, sem, held, sent):
    points, win = w.shape
    nblocks = corr.shape[1]
    per_row = a_all.shape[1] // win

    @pl.when(pl.program_id(0) == 0)
    def _():
        r, c = lax.axis_index("row"), lax.axis_index("col")
        off = pl.multiple_of((c % per_row) * win, win)
        is_root = r == c // per_row

        @pl.when(is_root)
        def _():
            pltpu.make_async_copy(a_all.at[:, pl.ds(off, win)], w, sem).start()

        @pl.when(jnp.logical_not(is_root))
        def _():
            pltpu.make_async_copy(w_all, w, sem).start()

        block = lax.broadcasted_iota(jnp.int32, (nblocks, points), 0)
        member = jnp.where(group[...] == block, 1.0, 0.0)
        spread = member.T
        scale = jnp.sum(spread * diag[...], axis=1, keepdims=True)
        member, spread = member.astype(jnp.bfloat16), spread.astype(jnp.bfloat16)
        square = (nblocks, nblocks)
        same = lax.broadcasted_iota(jnp.int32, square, 0) == lax.broadcasted_iota(jnp.int32, square, 1)
        weight = jnp.sum(jnp.where(same, corr[...], 0.0), axis=1, keepdims=True)
        pltpu.make_async_copy(w_all, w, sem).wait()
        wide = min(win, 512)
        for i in range(win // wide):
            cols = slice(i * wide, (i + 1) * wide)
            part = w[:, cols]
            sums = jnp.dot(member, part, preferred_element_type=jnp.float32).astype(jnp.bfloat16)
            rows = (weight * sums.astype(jnp.float32)).astype(jnp.bfloat16)
            back = jnp.dot(spread, rows, preferred_element_type=jnp.float32)
            scaled[:, cols] = (scale * part.astype(jnp.float32) + back).astype(jnp.bfloat16)

    step, steps = pl.program_id(0), pl.num_programs(0)
    tile = a.shape[1]
    slot = step % 2
    wide = min(win, 512)

    def store(at, i):
        cols = pl.ds(i * wide, wide)
        rows = pl.ds(pl.multiple_of(at * tile, tile), tile)
        return pltpu.make_async_copy(held.at[at % 2, :, cols], out.at[rows, cols], sent.at[at % 2, i])

    for i in range(win // wide):

        @pl.when(step >= 2)
        def _():
            store(step - 2, i).wait()

        cols = slice(i * wide, (i + 1) * wide)
        held[slot, :, cols] = lax.dot_general(
            a[...], scaled[:, cols], (((0,), (0,)), ((), ())), preferred_element_type=jnp.float32
        )
        store(step, i).start()

    @pl.when(step == steps - 1)
    def _():
        for i in range(win // wide):
            store(step - 1, i).wait()
            store(step, i).wait()


def local(jac, owner_list, block_id, diag_weight, corr_weight):
    n_row, n_col = lax.axis_size("row"), lax.axis_size("col")
    pt_dev, width = jac.shape
    points = owner_list.shape[0]
    block, win = width // n_row, width // n_col
    slots = n_row * n_col
    nblocks = diag_weight.shape[0]
    dma = pltpu.SemaphoreType.DMA
    a, w = pl.pallas_call(
        functools.partial(gather_kernel, n_col, block, win),
        out_shape=(
            jax.ShapeDtypeStruct((slots, pt_dev, block), jac.dtype),
            jax.ShapeDtypeStruct((slots, pt_dev, win), jac.dtype),
        ),
        in_specs=[pl.BlockSpec(memory_space=pl.ANY)],
        out_specs=(pl.BlockSpec(memory_space=pl.ANY), pl.BlockSpec(memory_space=pl.ANY)),
        scratch_shapes=[
            dma(()), dma((3,)), dma((n_row,)), dma((slots,)), dma((slots,)), dma((slots,)), dma((slots,)), dma((slots,)),
            dma((slots // 2,)), dma((slots // 2,)), dma((slots // 2,)), dma((slots,)), dma((slots,)),
        ],
        compiler_params=pltpu.CompilerParams(collective_id=0, has_side_effects=True),
        name="gather",
    )(jac)
    a = a.reshape(points, block)
    w = w.reshape(points, win)
    group = owner_list.reshape(1, points) * BPC + block_id.reshape(1, points)
    tile = 512
    whole = lambda *shape: pl.BlockSpec(shape, lambda i: (0, 0))
    return pl.pallas_call(
        product_kernel,
        grid=(block // tile,),
        out_shape=jax.ShapeDtypeStruct((block, win), jnp.float32),
        in_specs=[
            whole(1, points), whole(1, nblocks), whole(1, nblocks),
            pl.BlockSpec((points, tile), lambda i: (0, i)),
            pl.BlockSpec(memory_space=pl.ANY), pl.BlockSpec(memory_space=pl.ANY),
        ],
        out_specs=pl.BlockSpec(memory_space=pl.ANY),
        scratch_shapes=[pltpu.VMEM((points, win), jnp.bfloat16)] * 2
        + [dma(()), pltpu.VMEM((2, tile, win), jnp.float32), dma((2, max(1, win // 512)))],
        compiler_params=pltpu.CompilerParams(vmem_limit_bytes=56 * 1024 * 1024),
        cost_estimate=pl.CostEstimate(flops=2 * points * block * win, bytes_accessed=4 * block * win, transcendentals=0),
        name="product",
    )(group, diag_weight[None, :], corr_weight[None, :], a, a, w)


def solution(mesh):
    in_specs = (P(("row", "col"), None), P(), P(), P(), P())
    out_specs = P("row", "col")
    return jax.shard_map(local, mesh=mesh, in_specs=in_specs, out_specs=out_specs, check_vma=False)
```

```python
import functools

import jax
import jax.numpy as jnp
from jax import lax
from jax.experimental import pallas as pl
from jax.experimental.pallas import tpu as pltpu
from jax.sharding import PartitionSpec as P

BPC = 8
MESH = pl.DeviceIdType.MESH


def gather_kernel(n_col, block, win, jac, a, w, loc, s1, sn, rn, rb, rw, nr, nl, sr, sl, sy, sw, sx):
    length = n_col // 2
    r, c = lax.axis_index("row"), lax.axis_index("col")
    z, y = c // 2, c % 2
    r1 = r + 1 - 2 * (r % 2)
    r2 = (r + 2) % 4
    r3 = (r1 + 2) % 4
    root = c // (block // win)
    root1 = root + 1 - 2 * (root % 2)
    root2 = (root + 2) % 4
    off = pl.multiple_of((c % (block // win)) * win, win)
    is_root, is_relay = r == root, r == root2
    has_right, has_left = z < length - 1, z > 0
    right, left, across = c + 2, c - 2, c + 1 - 2 * y

    barrier = pltpu.get_barrier_semaphore()

    def greet(row, col):
        pl.semaphore_signal(barrier, inc=1, device_id=(row, col), device_id_type=MESH)

    for peer in (r1, r2, r3):
        greet(peer, c)
    greet(r, across)

    @pl.when(has_right)
    def _():
        greet(r, right)

    @pl.when(has_left)
    def _():
        greet(r, left)

    pl.semaphore_wait(barrier, 4 + jnp.where(has_right, 1, 0) + jnp.where(has_left, 1, 0))

    def remote(src, dst, send, recv, row, col):
        return pltpu.make_async_remote_copy(
            src_ref=src, dst_ref=dst, send_sem=send, recv_sem=recv, device_id=(row, col), device_id_type=MESH
        )

    mine = r * n_col + c
    own = pltpu.make_async_copy(jac.at[:, pl.ds(pl.multiple_of(r * block, block), block)], a.at[mine], loc)
    own.start()
    first = [
        remote(jac.at[:, pl.ds(pl.multiple_of(peer * block, block), block)], a.at[mine], s1.at[i], rb.at[mine], peer, c)
        for i, peer in enumerate((r1, r2, r3))
    ]
    for copy in (first[1], first[2], first[0]):
        copy.start()

    cut = block * 5 // 32
    near, far = pl.ds(0, cut), pl.ds(cut, block - cut)

    def n_copy(s, send, col):
        return remote(a.at[s, :, near], a.at[s, :, near], send, rn.at[s], r, col)

    def n_across(s):
        return n_copy(s, sn.at[s // n_col], across)

    def n_right(s):
        return n_copy(s, nr.at[s], right)

    def n_left(s):
        return n_copy(s, nl.at[s], left)

    def a_copy(s, sems, col):
        return remote(
            a.at[s, :, far], a.at[s, :, far], sems.at[s % n_col // 2 * 4 + s // n_col], rb.at[s], r, col
        )

    def a_wait(s):
        a_copy(s, sy, across).wait_recv()

    def w_copy(s, sems, row):
        return remote(a.at[s, :, pl.ds(off, win)], w.at[s], sems.at[s], rw.at[s], row, c)

    def w_relay(s):
        return remote(w.at[s], w.at[s], sw.at[s], rw.at[s], r1, c)

    def w_start(s):
        @pl.when(is_root)
        def _():
            w_copy(s, sx, root2).start()
            w_copy(s, sw, root1).start()

    def w_pass(s):
        @pl.when(is_relay)
        def _():
            w_relay(s).wait_recv()
            w_relay(s).start()

    def send_right(s):
        @pl.when(has_right)
        def _():
            a_copy(s, sr, right).start()

    def send_left(s):
        @pl.when(has_left)
        def _():
            a_copy(s, sl, left).start()

    def near_right(s):
        @pl.when(has_right)
        def _():
            n_right(s).start()

    def near_left(s):
        @pl.when(has_left)
        def _():
            n_left(s).start()

    def send_across(s):
        a_copy(s, sy, across).start()

    for j, k in enumerate((r, r1, r2, r3)):
        s = k * n_col + c
        if j == 0:
            own.wait()
        else:
            remote(a.at[s], a.at[s], s1.at[0], rb.at[s], r1, c).wait_recv()
        n_across(s).start()
        send_right(s)
        send_left(s)
        send_across(s)
        near_right(s)
        near_left(s)
        w_start(s)

    def both(d, k, lane, act_left, act_right, first_too):
        @pl.when((d >= (0 if first_too else 1)) & (d < length) & (z - d >= 0))
        def _():
            act_left(k * n_col + (z - d) * 2 + lane)

        @pl.when((d >= 1) & (d < length) & (z + d < length))
        def _():
            act_right(k * n_col + (z + d) * 2 + lane)

    def step(t, carry):
        d, j = t // 4, t % 4
        k = jnp.where(j == 0, r, jnp.where(j == 1, r1, jnp.where(j == 2, r2, r3)))

        def from_left(s):
            a_wait(s)
            send_right(s)
            send_across(s)
            n_across(s).wait_recv()
            near_right(s)
            w_start(s)

        def from_right(s):
            a_wait(s)
            send_left(s)
            send_across(s)
            n_across(s).wait_recv()
            near_left(s)
            w_start(s)

        def near_from_left(s):
            n_across(s).wait_recv()
            near_right(s)

            @pl.when(d == 1)
            def _():
                near_left(s)

        def near_from_right(s):
            n_across(s).wait_recv()
            near_left(s)

        def from_across(s):
            a_wait(s)
            w_start(s)

        both(d, k, y, from_left, from_right, False)
        both(d - 1, k, 1 - y, near_from_left, near_from_right, True)
        both(d - 1, k, 1 - y, from_across, from_across, True)
        both(d - 1, k, y, w_pass, w_pass, True)
        both(d - 2, k, 1 - y, w_pass, w_pass, True)
        return carry

    lax.fori_loop(4, (length + 2) * 4, step, 0)

    def finish(i, carry):
        zz, k = i // 4, i % 4
        s = k * n_col + zz * 2 + y
        a_copy(s, sy, across).wait_send()

        @pl.when(has_right & (zz <= z))
        def _():
            a_copy(s, sr, right).wait_send()

        @pl.when(has_left & (zz >= z))
        def _():
            a_copy(s, sl, left).wait_send()

        return carry

    lax.fori_loop(0, length * 4, finish, 0)

    for k in range(4):
        n_across(k * n_col + c).wait_send()

    def finish_w(s, carry):
        zz = s % n_col // 2

        @pl.when(has_right & (zz <= z))
        def _():
            n_right(s).wait_send()

        @pl.when(has_left & (zz >= z))
        def _():
            n_left(s).wait_send()

        @pl.when(is_root)
        def _():
            w_copy(s, sx, root2).wait_send()
            w_copy(s, sw, root1).wait_send()

        @pl.when(is_relay)
        def _():
            w_relay(s).wait_send()

        @pl.when(jnp.logical_not(is_root | is_relay))
        def _():
            w_relay(s).wait_recv()

        return carry

    lax.fori_loop(0, n_col * 4, finish_w, 0)
    for copy in first:
        copy.wait_send()


def product_kernel(owner, ident, diag, corr, a, a_all, w_all, out, w, scaled, sem):
    points, win = w.shape
    nblocks = corr.shape[1]
    per_row = a_all.shape[1] // win

    @pl.when(pl.program_id(0) == 0)
    def _():
        r, c = lax.axis_index("row"), lax.axis_index("col")
        off = pl.multiple_of((c % per_row) * win, win)
        is_root = r == c // per_row

        @pl.when(is_root)
        def _():
            pltpu.make_async_copy(a_all.at[:, pl.ds(off, win)], w, sem).start()

        @pl.when(jnp.logical_not(is_root))
        def _():
            pltpu.make_async_copy(w_all, w, sem).start()

        block = lax.broadcasted_iota(jnp.int32, (nblocks, points), 0)
        member = jnp.where(owner[...] * BPC + ident[...] == block, 1.0, 0.0)
        spread = member.T
        scale = jnp.sum(spread * diag[...], axis=1, keepdims=True)
        member, spread = member.astype(jnp.bfloat16), spread.astype(jnp.bfloat16)
        square = (nblocks, nblocks)
        same = lax.broadcasted_iota(jnp.int32, square, 0) == lax.broadcasted_iota(jnp.int32, square, 1)
        weight = jnp.sum(jnp.where(same, corr[...], 0.0), axis=1, keepdims=True)
        pltpu.make_async_copy(w_all, w, sem).wait()
        wide = min(win, 512)
        for i in range(win // wide):
            cols = slice(i * wide, (i + 1) * wide)
            part = w[:, cols]
            sums = jnp.dot(member, part, preferred_element_type=jnp.float32).astype(jnp.bfloat16)
            rows = (weight * sums.astype(jnp.float32)).astype(jnp.bfloat16)
            back = jnp.dot(spread, rows, preferred_element_type=jnp.float32)
            scaled[:, cols] = (scale * part.astype(jnp.float32) + back).astype(jnp.bfloat16)

    out[...] = lax.dot_general(
        a[...], scaled[...], (((0,), (0,)), ((), ())), preferred_element_type=jnp.float32
    )


def local(jac, owner_list, block_id, diag_weight, corr_weight):
    n_row, n_col = lax.axis_size("row"), lax.axis_size("col")
    pt_dev, width = jac.shape
    points = owner_list.shape[0]
    block, win = width // n_row, width // n_col
    slots = n_row * n_col
    nblocks = diag_weight.shape[0]
    dma = pltpu.SemaphoreType.DMA
    a, w = pl.pallas_call(
        functools.partial(gather_kernel, n_col, block, win),
        out_shape=(
            jax.ShapeDtypeStruct((slots, pt_dev, block), jac.dtype),
            jax.ShapeDtypeStruct((slots, pt_dev, win), jac.dtype),
        ),
        in_specs=[pl.BlockSpec(memory_space=pl.ANY)],
        out_specs=(pl.BlockSpec(memory_space=pl.ANY), pl.BlockSpec(memory_space=pl.ANY)),
        scratch_shapes=[
            dma(()), dma((3,)), dma((n_row,)), dma((slots,)), dma((slots,)), dma((slots,)), dma((slots,)), dma((slots,)),
            dma((slots // 2,)), dma((slots // 2,)), dma((slots // 2,)), dma((slots,)), dma((slots,)),
        ],
        compiler_params=pltpu.CompilerParams(collective_id=0, has_side_effects=True),
        name="gather",
    )(jac)
    a = a.reshape(points, block)
    w = w.reshape(points, win)
    tile = 512
    whole = lambda *shape: pl.BlockSpec(shape, lambda i: (0, 0))
    return pl.pallas_call(
        product_kernel,
        grid=(block // tile,),
        out_shape=jax.ShapeDtypeStruct((block, win), jnp.float32),
        in_specs=[
            whole(1, points), whole(1, points), whole(1, nblocks), whole(1, nblocks),
            pl.BlockSpec((points, tile), lambda i: (0, i)),
            pl.BlockSpec(memory_space=pl.ANY), pl.BlockSpec(memory_space=pl.ANY),
        ],
        out_specs=pl.BlockSpec((tile, win), lambda i: (i, 0)),
        scratch_shapes=[pltpu.VMEM((points, win), jnp.bfloat16)] * 2 + [dma(())],
        compiler_params=pltpu.CompilerParams(vmem_limit_bytes=56 * 1024 * 1024),
        cost_estimate=pl.CostEstimate(flops=2 * points * block * win, bytes_accessed=4 * block * win, transcendentals=0),
        name="product",
    )(owner_list.reshape(1, points), block_id.reshape(1, points), diag_weight[None, :], corr_weight[None, :], a, a, w)


def solution(mesh):
    in_specs = (P(("row", "col"), None), P(), P(), P(), P())
    out_specs = P("row", "col")
    return jax.shard_map(local, mesh=mesh, in_specs=in_specs, out_specs=out_specs, check_vma=False)
```
